512 devices in a mesh: rep: 8 (over z_lo), fsdp: 16 (over z_hi, y, core), tp: 4 (over x).
Axes of the slice: x: 4, y: 4, z: 16 (z_hi: 2, z_lo: 8; z = z_hi * 8 + z_lo), core: 2. Of those that a mesh axis runs over, the one named last changes fastest.
Arguments:
- local_params: bfloat16 [8, 256, 32768], P('rep', 'fsdp', 'tp'), may hold values from -6 to 6
- global_owned: float32 [16, 16, 32768], P('rep', 'fsdp', 'tp'), may hold values from -6 to 6
- momentum: float32 [16, 16, 32768], P('rep', 'fsdp', 'tp'), may hold values from -4 to 4
Outputs:
- global_next: float32 [16, 16, 32768], P('rep', 'fsdp', 'tp')
- momentum_next: float32 [16, 16, 32768], P('rep', 'fsdp', 'tp')
- replica_params: bfloat16 [256, 32768], P('fsdp', 'tp')
The draws below stay inside these ranges and needn't reach their ends.
All inputs are finite; a program needn't handle non-finite values.
Results may differ from the reference program's by a relative error of at most 0.015.
Values may be sent and summed in bfloat16 or wider, within the bound.
No kernel may reach another device: no remote copies, remote signals or barrier semaphores. Data moves between devices by JAX's collectives and lax.ppermute only.
A program may use at most 192 MiB of HBM per device.

```python
import jax
import jax.numpy as jnp

COLS = 32768
ROW_BLOCK = 16
ROWS = 256
N_REP = 8
N_FSDP = 16


def levels(stream_key, dims, split, low, top_value):
    level = 1.0
    for axis_at, parts in split:
        steps = jax.random.uniform(jax.random.fold_in(jax.random.fold_in(stream_key, 6), axis_at), (parts,), jnp.float32, low / len(split), top_value / len(split))
        level = level * jnp.repeat(jnp.exp(steps), dims[axis_at] // parts).reshape((-1,) + (1,) * (len(dims) - 1 - axis_at))
    return level


def scatter_about(own_key, extent, scale, reach, shards=(), held_as=jnp.bfloat16):
    factor_of = levels(own_key, extent, shards, -0.22, 0.18) if shards else 1.0
    values = jax.random.normal(own_key, extent, jnp.float32) * scale * factor_of
    return jnp.minimum(jnp.maximum(values, -reach), reach).astype(held_as)


def setup_inputs(seed: int = 0) -> dict:
    key_list = jax.random.split(jax.random.key(seed), 4)
    return {
        "local_params": scatter_about(key_list[0], (N_REP, ROWS, COLS), 1.0, 6.0, ((0, 8), (1, 16), (2, 4))),
        "global_owned": scatter_about(key_list[1], (N_FSDP, ROW_BLOCK, COLS), 1.0, 6.0, ((0, 8), (1, 16), (2, 4)), jnp.float32),
        "momentum": scatter_about(key_list[2], (N_FSDP, ROW_BLOCK, COLS), 0.5, 4.0, ((0, 8), (1, 16), (2, 4)), jnp.float32),
    }


def reference(local_params, global_owned, momentum):
    mean_local = jnp.sum(local_params, axis=0, dtype=jnp.float32) / N_REP
    global_rows = global_owned.reshape(ROWS, COLS)
    moment_rows = momentum.reshape(ROWS, COLS)
    pseudo_grad = global_rows - mean_local
    moment_new = 0.9 * moment_rows + pseudo_grad
    global_new = global_rows - 0.7 * (pseudo_grad + 0.9 * moment_new)
    replica_params = global_new.astype(jnp.bfloat16)
    return (global_new.reshape(N_FSDP, ROW_BLOCK, COLS), moment_new.reshape(N_FSDP, ROW_BLOCK, COLS), replica_params)
```

```python
import jax
import jax.numpy as jnp
from jax import lax
from jax.sharding import PartitionSpec as P

AXES = ("rep", "fsdp")
BOTH = 8


def spot(half, quad, col, core):
    return (half * 4 + quad) * 16 + col * 2 + core


def each():
    return [(h, j, c, k) for h in range(2) for j in range(4) for c in range(8) for k in range(2)]


QUAD_CORE = [
    [spot(h, j, c, k) for j in range(4) for k in range(2)] for h in range(2) for c in range(8)
]
CROSS = [(spot(h, j, c, k), spot(1 - h, j, c, k)) for h, j, c, k in each()]
TURN = [(spot(h, j, c, k), spot(c // 4, c % 4, h * 4 + j, k)) for h, j, c, k in each()]
TURN_FLIP = [(spot(h, j, c, k), spot(1 - c // 4, c % 4, h * 4 + j, k)) for h, j, c, k in each()]


def body(local_params, global_owned, momentum):
    width = local_params.shape[2]
    half = lax.axis_index("rep") // 4
    owned = global_owned[:, 0]
    moment = momentum[:, 0]
    state = lax.reduce_precision(-0.33 * owned - 0.567 * moment, 8, 7).astype(jnp.bfloat16)

    blocks = local_params[0].reshape(2, 8, width).transpose(1, 0, 2)
    got = lax.all_to_all(blocks, AXES, split_axis=0, concat_axis=0, tiled=True, axis_index_groups=QUAD_CORE)
    part = jnp.sum(got.reshape(4, 2, 2, width).astype(jnp.float32), axis=0)
    part = lax.reduce_precision(part, 8, 7).astype(jnp.bfloat16)
    other = lax.ppermute(part, AXES, CROSS)
    state_same = lax.ppermute(state, AXES, TURN)
    state_flip = lax.ppermute(state, AXES, TURN_FLIP_A)
    summed = part.astype(jnp.float32) + other.astype(jnp.float32)
    s0 = jnp.where(half == 0, state_same, state_flip)
    s1 = jnp.where(half == 0, state_flip, state_same)
    states = jnp.stack([s0, s1], axis=1).astype(jnp.float32)
    fresh = (states + (1.33 / 8) * summed).astype(jnp.bfloat16)
    mine = jnp.where(half == 0, summed[:, 0], summed[:, 1]).astype(jnp.bfloat16)
    back = lax.ppermute(mine, AXES, TURN)

    spread = jnp.broadcast_to(fresh[None], (4, 2, 2, width)).reshape(8, 2, width)
    rows = lax.all_to_all(spread, AXES, split_axis=0, concat_axis=0, tiled=True, axis_index_groups=QUAD_CORE)
    replica_params = rows.transpose(1, 0, 2).reshape(16, width)

    mean_local = back.astype(jnp.float32) / 8
    pseudo = owned - mean_local
    moment_new = 0.9 * moment + pseudo
    global_new = owned - 0.7 * (pseudo + 0.9 * moment_new)
    return (global_new[:, None], moment_new[:, None], replica_params)


TURN_FLIP_A = [(spot(a, b, zy, k), spot(1 - zy // 4, zy % 4, a * 4 + b, k)) for a, b, zy, k in each()]


def solution(mesh):
    return jax.shard_map(
        body,
        mesh=mesh,
        in_specs=(P("rep", "fsdp", "tp"), P("rep", "fsdp", "tp"), P("rep", "fsdp", "tp")),
        out_specs=(P("rep", "fsdp", "tp"), P("rep", "fsdp", "tp"), P("fsdp", "tp")),
        check_vma=False,
    )
```

```python
import jax
import jax.numpy as jnp
from jax import lax
from jax.sharding import PartitionSpec as P

AXES = ("rep", "fsdp")
SHARE = 1.33 / 8


def spot(half, quad, col, core):
    return (half * 4 + quad) * 16 + col * 2 + core


EACH = [(h, j, c, k) for h in range(2) for j in range(4) for c in range(8) for k in range(2)]
QUAD_CORE = [
    [spot(h, j, c, k) for j in range(4) for k in range(2)] for h in range(2) for c in range(8)
]
CROSS = [(spot(h, j, c, k), spot(1 - h, j, c, k)) for h, j, c, k in EACH]
TURN = [(spot(h, j, c, k), spot(c // 4, c % 4, h * 4 + j, k)) for h, j, c, k in EACH]
FLIP = [(spot(h, j, c, k), spot(1 - c // 4, c % 4, h * 4 + j, k)) for h, j, c, k in EACH]


def rounded(x):
    return lax.reduce_precision(x, 8, 7).astype(jnp.bfloat16)


def spread(x):
    return lax.all_to_all(x, AXES, split_axis=0, concat_axis=0, tiled=True, axis_index_groups=QUAD_CORE)


def body(local_params, global_owned, momentum):
    width = local_params.shape[2]
    deep = (width // 128, 128)
    half = (lax.axis_index("rep") // 4).astype(jnp.int32)
    owned = global_owned.reshape(2, *deep)
    moment = momentum.reshape(2, *deep)
    f32 = jnp.float32

    blocks = local_params[0].reshape(2, 8, *deep).transpose(1, 0, 2, 3)
    got = spread(blocks)
    state = rounded(-0.33 * owned - 0.567 * moment)
    flipped = lax.ppermute(state, AXES, FLIP).astype(f32)
    held = lax.ppermute(state, AXES, TURN).astype(f32)
    part = rounded(jnp.sum(got.reshape(4, 2, 2, *deep).astype(f32), axis=0))
    other = lax.ppermute(part, AXES, CROSS)
    total = lax.optimization_barrier(part.astype(f32) + other.astype(f32))
    here = (lax.iota(jnp.int32, 2) == half)[None, :, None, None]
    fresh = (SHARE * total + jnp.where(here, held[:, None], flipped[:, None])).astype(jnp.bfloat16)
    rows = spread(jnp.broadcast_to(fresh[None], (4, 2, 2, *deep)).reshape(8, 2, *deep))
    mine = rounded(jnp.where(half == 0, total[:, 0], total[:, 1]))
    back = lax.ppermute(mine, AXES, TURN)

    replica_params = rows.transpose(1, 0, 2, 3).reshape(16, width)
    back, owned, moment = lax.optimization_barrier((back, owned, moment))
    pseudo = owned - back.astype(f32) / 8
    moment_new = 0.9 * moment + pseudo
    global_new = owned - 0.7 * (pseudo + 0.9 * moment_new)
    return (global_new.reshape(2, 1, width), moment_new.reshape(2, 1, width), replica_params)


def solution(mesh):
    return jax.shard_map(
        body,
        mesh=mesh,
        in_specs=(P("rep", "fsdp", "tp"), P("rep", "fsdp", "tp"), P("rep", "fsdp", "tp")),
        out_specs=(P("rep", "fsdp", "tp"), P("rep", "fsdp", "tp"), P("fsdp", "tp")),
        check_vma=False,
    )
```

```python
import jax
import jax.numpy as jnp
from jax import lax
from jax.sharding import PartitionSpec as P

AXES = ("rep", "fsdp")
SHARE = 1.33 / 8


def spot(rep, col, core):
    return rep * 16 + col * 2 + core


EACH = [(b, c, k) for b in range(8) for c in range(8) for k in range(2)]
LINE = [
    [spot(r, c, k) for y in range(4) for r in (4 + y, 3 - y) for k in range(2)] for c in range(8)
]
HOLDER = [3 - b if b < 4 else b for b in range(8)]
TO_HOLDER = [(spot(c, b, k), spot(HOLDER[b], c, k)) for b, c, k in EACH]
TO_OWNER = [(b, a) for a, b in TO_HOLDER]


def rounded(x):
    return lax.reduce_precision(x, 8, 7).astype(jnp.bfloat16)


def swap_rows(x):
    return lax.all_to_all(x, AXES, split_axis=0, concat_axis=0, tiled=True, axis_index_groups=LINE)


def body(local_params, global_owned, momentum):
    rows, width = local_params.shape[1:]
    deep = (width // 128, 128)
    owned = global_owned.reshape(2, *deep)
    moment = momentum.reshape(2, *deep)
    f32 = jnp.float32

    blocks = local_params[0].reshape(2, 4, 2, *deep)[::-1].transpose(1, 0, 2, 3, 4)
    got = swap_rows(blocks.reshape(rows, *deep))
    state = rounded(-0.33 * owned - 0.567 * moment)
    held = lax.ppermute(state, AXES, TO_HOLDER).astype(f32)
    summed = jnp.sum(got.reshape(8, 2, *deep).astype(f32), axis=0)
    fresh = (held + SHARE * summed).astype(jnp.bfloat16)
    back = lax.ppermute(rounded(summed), AXES, TO_OWNER)
    spread = jnp.broadcast_to(fresh[None], (8, 2, *deep)).reshape(rows, *deep)
    out = swap_rows(spread).reshape(4, 2, 2, *deep).transpose(1, 0, 2, 3, 4)[::-1]
    replica_params = out.reshape(rows, width)

    back, owned, moment = lax.optimization_barrier((back, owned, moment))
    pseudo = owned - back.astype(f32) / 8
    moment_new = 0.9 * moment + pseudo
    global_new = owned - 0.7 * (pseudo + 0.9 * moment_new)
    return (global_new.reshape(2, 1, width), moment_new.reshape(2, 1, width), replica_params)


def solution(mesh):
    return jax.shard_map(
        body,
        mesh=mesh,
        in_specs=(P("rep", "fsdp", "tp"), P("rep", "fsdp", "tp"), P("rep", "fsdp", "tp")),
        out_specs=(P("rep", "fsdp", "tp"), P("rep", "fsdp", "tp"), P("fsdp", "tp")),
        check_vma=False,
    )
```

```python
import jax
import jax.numpy as jnp
from jax import lax
from jax.sharding import PartitionSpec as P

AXES = ("rep", "fsdp")
SHARE = 1.33 / 8
UPPER = ((4, 7, 5, 6), (4, 5, 6, 7))
LOWER = (((0, 3, 2, 1), (3, 2, 1, 0)), ((3, 2, 1, 0), (0, 1, 2, 3)))


def spot(rep, col, core):
    return rep * 16 + col * 2 + core


def holder(block, col, core):
    side = col // 4
    rep = UPPER[side][block - 4] if block >= 4 else LOWER[side][core][block]
    return spot(rep, col, core)


LINE = [
    [holder(block, c, k) for y in range(4) for block in (4 + y, y) for k in (1, 0)] for c in range(8)
]
TO_HOLDER = [
    (spot(c, block, k), holder(block, c, k)) for block in range(8) for c in range(8) for k in range(2)
]
TO_OWNER = [(b, a) for a, b in TO_HOLDER]


def rounded(x):
    return lax.reduce_precision(x, 8, 7).astype(jnp.bfloat16)


def swap_rows(x):
    return lax.all_to_all(x, AXES, split_axis=0, concat_axis=0, tiled=True, axis_index_groups=LINE)


def body(local_params, global_owned, momentum):
    rows, width = local_params.shape[1:]
    deep = (width // 128, 128)
    owned = global_owned.reshape(2, *deep)
    moment = momentum.reshape(2, *deep)
    f32 = jnp.float32

    blocks = local_params[0].reshape(2, 4, 2, *deep)[::-1, :, ::-1].transpose(1, 0, 2, 3, 4)
    got = swap_rows(blocks.reshape(rows, *deep))
    state = rounded(-0.33 * owned - 0.567 * moment)
    held = lax.ppermute(state, AXES, TO_HOLDER).astype(f32)
    summed = jnp.sum(got.reshape(8, 2, *deep).astype(f32), axis=0)[::-1]
    fresh = (held + SHARE * summed).astype(jnp.bfloat16)
    back = lax.ppermute(rounded(summed), AXES, TO_OWNER)
    spread = jnp.broadcast_to(fresh[None, ::-1], (8, 2, *deep)).reshape(rows, *deep)
    out = swap_rows(spread).reshape(4, 2, 2, *deep).transpose(1, 0, 2, 3, 4)[::-1, :, ::-1]
    replica_params = out.reshape(rows, width)

    back, owned, moment = lax.optimization_barrier((back, owned, moment))
    pseudo = owned - back.astype(f32) / 8
    moment_new = 0.9 * moment + pseudo
    global_new = owned - 0.7 * (pseudo + 0.9 * moment_new)
    return (global_new.reshape(2, 1, width), moment_new.reshape(2, 1, width), replica_params)


def solution(mesh):
    return jax.shard_map(
        body,
        mesh=mesh,
        in_specs=(P("rep", "fsdp", "tp"), P("rep", "fsdp", "tp"), P("rep", "fsdp", "tp")),
        out_specs=(P("rep", "fsdp", "tp"), P("rep", "fsdp", "tp"), P("fsdp", "tp")),
        check_vma=False,
    )
```

```python
import jax
import jax.numpy as jnp
from jax import lax
from jax.experimental import pallas as pl
from jax.experimental.pallas import tpu as pltpu
from jax.sharding import PartitionSpec as P

AXES = ("rep", "fsdp")
SHARE = 1.33 / 8
UPPER = ((4, 7, 5, 6), (4, 5, 6, 7))
LOWER = (((0, 3, 2, 1), (3, 2, 1, 0)), ((3, 2, 1, 0), (0, 1, 2, 3)))


def spot(rep, col, core):
    return rep * 16 + col * 2 + core


def holder(block, col, core):
    side = col // 4
    rep = UPPER[side][block - 4] if block >= 4 else LOWER[side][core][block]
    return spot(rep, col, core)


LINE = [
    [holder(block, c, k) for y in range(4) for block in (4 + y, y) for k in (1, 0)] for c in range(8)
]
TO_HOLDER = [
    (spot(c, block, k), holder(block, c, k)) for block in range(8) for c in range(8) for k in range(2)
]
TO_OWNER = [(b, a) for a, b in TO_HOLDER]


def rounded(x):
    return lax.reduce_precision(x, 8, 7).astype(jnp.bfloat16)


def swap_rows(x):
    return lax.all_to_all(x, AXES, split_axis=0, concat_axis=0, tiled=True, axis_index_groups=LINE)


def fresh_kernel(got_ref, held_ref, spread_ref, sums_ref):
    f32 = jnp.float32
    for core in range(2):
        summed = got_ref[0, 1 - core].astype(f32)
        for i in range(1, 8):
            summed = summed + got_ref[i, 1 - core].astype(f32)
        sums_ref[core] = summed.astype(jnp.bfloat16)
        fresh = (held_ref[core].astype(f32) + SHARE * summed).astype(jnp.bfloat16)
        for i in range(8):
            spread_ref[i, 1 - core] = fresh


def fresh_rows(got, held):
    vmem = pl.BlockSpec(memory_space=pltpu.VMEM)
    got = pltpu.with_memory_space_constraint(got, pltpu.VMEM)
    held = pltpu.with_memory_space_constraint(held, pltpu.VMEM)
    return pl.pallas_call(
        fresh_kernel,
        out_shape=[pltpu.VMEM(got.shape, got.dtype), pltpu.VMEM(held.shape, held.dtype)],
        in_specs=[vmem] * 2,
        out_specs=[vmem] * 2,
        compiler_params=pltpu.CompilerParams(vmem_limit_bytes=4 * 2**20),
    )(got, held)


def body(local_params, global_owned, momentum):
    rows, width = local_params.shape[1:]
    deep = (width // 128, 128)
    owned = global_owned.reshape(2, *deep)
    moment = momentum.reshape(2, *deep)
    f32 = jnp.float32

    blocks = local_params[0].reshape(2, 4, 2, *deep)[::-1, :, ::-1].transpose(1, 0, 2, 3, 4)
    got = swap_rows(blocks.reshape(rows, *deep))
    state = rounded(-0.33 * owned - 0.567 * moment)
    held = lax.ppermute(state, AXES, TO_HOLDER)
    spread, sums = fresh_rows(got.reshape(8, 2, *deep), held)
    back = lax.ppermute(sums, AXES, TO_OWNER)
    spread = spread.reshape(rows, *deep)
    out = swap_rows(spread).reshape(4, 2, 2, *deep).transpose(1, 0, 2, 3, 4)[::-1, :, ::-1]
    replica_params = out.reshape(rows, width)

    back, owned, moment = lax.optimization_barrier((back, owned, moment))
    pseudo = owned - back.astype(f32) / 8
    moment_new = 0.9 * moment + pseudo
    global_new = owned - 0.7 * (pseudo + 0.9 * moment_new)
    return (global_new.reshape(2, 1, width), moment_new.reshape(2, 1, width), replica_params)


def solution(mesh):
    return jax.shard_map(
        body,
        mesh=mesh,
        in_specs=(P("rep", "fsdp", "tp"), P("rep", "fsdp", "tp"), P("rep", "fsdp", "tp")),
        out_specs=(P("rep", "fsdp", "tp"), P("rep", "fsdp", "tp"), P("fsdp", "tp")),
        check_vma=False,
    )
```

```python
import jax
import jax.numpy as jnp
from jax import lax
from jax.experimental import pallas as pl
from jax.experimental.pallas import tpu as pltpu
from jax.sharding import PartitionSpec as P

AXES = ("rep", "fsdp")
SHARE = 1.33 / 8
UPPER = ((4, 7, 5, 6), (4, 5, 6, 7))
LOWER = (((0, 3, 2, 1), (3, 2, 1, 0)), ((3, 2, 1, 0), (0, 1, 2, 3)))


def spot(rep, col, core):
    return rep * 16 + col * 2 + core


def holder(block, col, core):
    side = col // 4
    rep = UPPER[side][block - 4] if block >= 4 else LOWER[side][core][block]
    return spot(rep, col, core)


LINE = [
    [holder(block, c, k) for y in range(4) for block in (4 + y, y) for k in (1, 0)] for c in range(8)
]
TO_HOLDER = [
    (spot(c, block, k), holder(block, c, k)) for block in range(8) for c in range(8) for k in range(2)
]
TO_OWNER = [(b, a) for a, b in TO_HOLDER]


def rounded(x):
    return lax.reduce_precision(x, 8, 7).astype(jnp.bfloat16)


def swap_rows(x):
    return lax.all_to_all(x, AXES, split_axis=0, concat_axis=0, tiled=True, axis_index_groups=LINE)


LISTED = [(4 * upper + y) * 2 + core for y in range(4) for upper in (1, 0) for core in (1, 0)]


PIECES = 4


def listed_kernel(rows_ref, out_ref, taken, listed, in_sems, out_sems):
    wide = rows_ref.shape[1] // PIECES
    deep = out_ref.shape[1] // PIECES
    fetches = [
        pltpu.make_async_copy(rows_ref.at[:, pl.ds(i * wide, wide)], taken.at[i], in_sems.at[i])
        for i in range(PIECES)
    ]
    stores = [
        pltpu.make_async_copy(listed.at[i], out_ref.at[:, pl.ds(i * deep, deep), :], out_sems.at[i])
        for i in range(PIECES)
    ]
    for fetch in fetches:
        fetch.start()
    for i in range(PIECES):
        fetches[i].wait()
        rows = taken[i].reshape(rows_ref.shape[0], deep, 128)
        for place, row in enumerate(LISTED):
            listed[i, place] = rows[row]
        stores[i].start()
    for store in stores:
        store.wait()


def listed_rows(rows, deep):
    anywhere = pl.BlockSpec(memory_space=pl.ANY)
    count, width = rows.shape
    return pl.pallas_call(
        listed_kernel,
        out_shape=jax.ShapeDtypeStruct((count,) + deep, rows.dtype),
        in_specs=[anywhere],
        out_specs=anywhere,
        scratch_shapes=[
            pltpu.VMEM((PIECES, count, width // PIECES), rows.dtype),
            pltpu.VMEM((PIECES, count, deep[0] // PIECES, 128), rows.dtype),
            pltpu.SemaphoreType.DMA((PIECES,)),
            pltpu.SemaphoreType.DMA((PIECES,)),
        ],
    )(rows)


def plain_kernel(listed_ref, out_ref, plain, sems):
    wide = out_ref.shape[1] // PIECES
    deep = listed_ref.shape[1] // PIECES
    stores = []
    for i in range(PIECES):
        rows = [listed_ref[LISTED.index(row), i * deep : (i + 1) * deep] for row in range(len(LISTED))]
        plain[i] = jnp.stack(rows).reshape(len(LISTED), wide)
        stores.append(
            pltpu.make_async_copy(plain.at[i], out_ref.at[:, pl.ds(i * wide, wide)], sems.at[i])
        )
        stores[-1].start()
    for store in stores:
        store.wait()


def plain_rows(listed):
    count, deep, _ = listed.shape
    listed = pltpu.with_memory_space_constraint(listed, pltpu.VMEM)
    return pl.pallas_call(
        plain_kernel,
        out_shape=jax.ShapeDtypeStruct((count, deep * 128), listed.dtype),
        in_specs=[pl.BlockSpec(memory_space=pltpu.VMEM)],
        out_specs=pl.BlockSpec(memory_space=pl.ANY),
        scratch_shapes=[
            pltpu.VMEM((PIECES, count, deep * 128 // PIECES), listed.dtype),
            pltpu.SemaphoreType.DMA((PIECES,)),
        ],
        compiler_params=pltpu.CompilerParams(vmem_limit_bytes=4 * 2**20),
    )(listed)


def fresh_kernel(got_ref, held_ref, spread_ref, sums_ref):
    f32 = jnp.float32
    for core in range(2):
        summed = got_ref[0, 1 - core].astype(f32)
        for i in range(1, 8):
            summed = summed + got_ref[i, 1 - core].astype(f32)
        sums_ref[core] = summed.astype(jnp.bfloat16)
        fresh = (held_ref[core].astype(f32) + SHARE * summed).astype(jnp.bfloat16)
        for i in range(8):
            spread_ref[i, 1 - core] = fresh


def fresh_rows(got, held):
    vmem = pl.BlockSpec(memory_space=pltpu.VMEM)
    got = pltpu.with_memory_space_constraint(got, pltpu.VMEM)
    held = pltpu.with_memory_space_constraint(held, pltpu.VMEM)
    return pl.pallas_call(
        fresh_kernel,
        out_shape=[pltpu.VMEM(got.shape, got.dtype), pltpu.VMEM(held.shape, held.dtype)],
        in_specs=[vmem] * 2,
        out_specs=[vmem] * 2,
        compiler_params=pltpu.CompilerParams(vmem_limit_bytes=4 * 2**20),
    )(got, held)


def body(local_params, global_owned, momentum):
    rows, width = local_params.shape[1:]
    deep = (width // 128, 128)
    owned = global_owned.reshape(2, *deep)
    moment = momentum.reshape(2, *deep)
    f32 = jnp.float32

    got = swap_rows(listed_rows(local_params[0], deep))
    state = rounded(-0.33 * owned - 0.567 * moment)
    held = lax.ppermute(state, AXES, TO_HOLDER)
    spread, sums = fresh_rows(got.reshape(8, 2, *deep), held)
    back = lax.ppermute(sums, AXES, TO_OWNER)
    spread = spread.reshape(rows, *deep)
    replica_params = plain_rows(swap_rows(spread))

    back, owned, moment = lax.optimization_barrier((back, owned, moment))
    pseudo = owned - back.astype(f32) / 8
    moment_new = 0.9 * moment + pseudo
    global_new = owned - 0.7 * (pseudo + 0.9 * moment_new)
    return (global_new.reshape(2, 1, width), moment_new.reshape(2, 1, width), replica_params)


def solution(mesh):
    return jax.shard_map(
        body,
        mesh=mesh,
        in_specs=(P("rep", "fsdp", "tp"), P("rep", "fsdp", "tp"), P("rep", "fsdp", "tp")),
        out_specs=(P("rep", "fsdp", "tp"), P("rep", "fsdp", "tp"), P("fsdp", "tp")),
        check_vma=False,
    )
```

```python
import jax
import jax.numpy as jnp
from jax import lax
from jax.experimental import pallas as pl
from jax.experimental.pallas import tpu as pltpu
from jax.sharding import PartitionSpec as P

AXES = ("rep", "fsdp")
SHARE = 1.33 / 8
UPPER = ((4, 7, 5, 6), (4, 5, 6, 7))
LOWER = (((0, 3, 2, 1), (3, 1, 2, 0)), ((3, 2, 1, 0), (0, 1, 2, 3)))


def spot(rep, col, core):
    return rep * 16 + col * 2 + core


def holder(block, col, core):
    side = col // 4
    rep = UPPER[side][block - 4] if block >= 4 else LOWER[side][core][block]
    return spot(rep, col, core)


LINE = [
    [holder(block, c, k) for y in range(4) for block in (4 + y, y) for k in (1, 0)] for c in range(8)
]
TO_HOLDER = [
    (spot(c, block, k), holder(block, c, k)) for block in range(8) for c in range(8) for k in range(2)
]
TO_OWNER = [(b, a) for a, b in TO_HOLDER]


def rounded(x):
    return lax.reduce_precision(x, 8, 7).astype(jnp.bfloat16)


def swap_rows(x):
    return lax.all_to_all(x, AXES, split_axis=0, concat_axis=0, tiled=True, axis_index_groups=LINE)


LISTED = [(4 * upper + y) * 2 + core for y in range(4) for upper in (1, 0) for core in (1, 0)]


PIECES = 4


def listed_kernel(rows_ref, out_ref, taken, listed, in_sems, out_sems):
    wide = rows_ref.shape[1] // PIECES
    deep = out_ref.shape[1] // PIECES
    fetches = [
        pltpu.make_async_copy(rows_ref.at[:, pl.ds(i * wide, wide)], taken.at[i], in_sems.at[i])
        for i in range(PIECES)
    ]
    stores = [
        pltpu.make_async_copy(listed.at[i], out_ref.at[:, pl.ds(i * deep, deep), :], out_sems.at[i])
        for i in range(PIECES)
    ]
    for fetch in fetches:
        fetch.start()
    for i in range(PIECES):
        fetches[i].wait()
        rows = taken[i].reshape(rows_ref.shape[0], deep, 128)
        for place, row in enumerate(LISTED):
            listed[i, place] = rows[row]
        stores[i].start()
    for store in stores:
        store.wait()


def listed_rows(rows, deep):
    anywhere = pl.BlockSpec(memory_space=pl.ANY)
    count, width = rows.shape
    return pl.pallas_call(
        listed_kernel,
        out_shape=jax.ShapeDtypeStruct((count,) + deep, rows.dtype),
        in_specs=[anywhere],
        out_specs=anywhere,
        scratch_shapes=[
            pltpu.VMEM((PIECES, count, width // PIECES), rows.dtype),
            pltpu.VMEM((PIECES, count, deep[0] // PIECES, 128), rows.dtype),
            pltpu.SemaphoreType.DMA((PIECES,)),
            pltpu.SemaphoreType.DMA((PIECES,)),
        ],
    )(rows)


def plain_kernel(listed_ref, out_ref, plain, sems):
    wide = out_ref.shape[1] // PIECES
    deep = listed_ref.shape[1] // PIECES
    stores = []
    for i in range(PIECES):
        rows = [listed_ref[LISTED.index(row), i * deep : (i + 1) * deep] for row in range(len(LISTED))]
        plain[i] = jnp.stack(rows).reshape(len(LISTED), wide)
        stores.append(
            pltpu.make_async_copy(plain.at[i], out_ref.at[:, pl.ds(i * wide, wide)], sems.at[i])
        )
        stores[-1].start()
    for store in stores:
        store.wait()


def plain_rows(listed):
    count, deep, _ = listed.shape
    listed = pltpu.with_memory_space_constraint(listed, pltpu.VMEM)
    return pl.pallas_call(
        plain_kernel,
        out_shape=jax.ShapeDtypeStruct((count, deep * 128), listed.dtype),
        in_specs=[pl.BlockSpec(memory_space=pltpu.VMEM)],
        out_specs=pl.BlockSpec(memory_space=pl.ANY),
        scratch_shapes=[
            pltpu.VMEM((PIECES, count, deep * 128 // PIECES), listed.dtype),
            pltpu.SemaphoreType.DMA((PIECES,)),
        ],
        compiler_params=pltpu.CompilerParams(vmem_limit_bytes=4 * 2**20),
    )(listed)


def fresh_kernel(got_ref, held_ref, spread_ref, sums_ref):
    f32 = jnp.float32
    for core in range(2):
        summed = got_ref[0, 1 - core].astype(f32)
        for i in range(1, 8):
            summed = summed + got_ref[i, 1 - core].astype(f32)
        sums_ref[core] = summed.astype(jnp.bfloat16)
        fresh = (held_ref[core].astype(f32) + SHARE * summed).astype(jnp.bfloat16)
        for i in range(8):
            spread_ref[i, 1 - core] = fresh


def fresh_rows(got, held):
    vmem = pl.BlockSpec(memory_space=pltpu.VMEM)
    got = pltpu.with_memory_space_constraint(got, pltpu.VMEM)
    held = pltpu.with_memory_space_constraint(held, pltpu.VMEM)
    return pl.pallas_call(
        fresh_kernel,
        out_shape=[pltpu.VMEM(got.shape, got.dtype), pltpu.VMEM(held.shape, held.dtype)],
        in_specs=[vmem] * 2,
        out_specs=[vmem] * 2,
        compiler_params=pltpu.CompilerParams(vmem_limit_bytes=4 * 2**20),
    )(got, held)


def body(local_params, global_owned, momentum):
    rows, width = local_params.shape[1:]
    deep = (width // 128, 128)
    owned = global_owned.reshape(2, *deep)
    moment = momentum.reshape(2, *deep)
    f32 = jnp.float32

    got = swap_rows(listed_rows(local_params[0], deep))
    state = rounded(-0.33 * owned - 0.567 * moment)
    held = lax.ppermute(state, AXES, TO_HOLDER)
    spread, sums = fresh_rows(got.reshape(8, 2, *deep), held)
    back = lax.ppermute(sums, AXES, TO_OWNER)
    spread = spread.reshape(rows, *deep)
    replica_params = plain_rows(swap_rows(spread))

    back, owned, moment = lax.optimization_barrier((back, owned, moment))
    pseudo = owned - back.astype(f32) / 8
    moment_new = 0.9 * moment + pseudo
    global_new = owned - 0.7 * (pseudo + 0.9 * moment_new)
    return (global_new.reshape(2, 1, width), moment_new.reshape(2, 1, width), replica_params)


def solution(mesh):
    return jax.shard_map(
        body,
        mesh=mesh,
        in_specs=(P("rep", "fsdp", "tp"), P("rep", "fsdp", "tp"), P("rep", "fsdp", "tp")),
        out_specs=(P("rep", "fsdp", "tp"), P("rep", "fsdp", "tp"), P("fsdp", "tp")),
        check_vma=False,
    )
```

```python
import jax
import jax.numpy as jnp
from jax import lax
from jax.experimental import pallas as pl
from jax.experimental.pallas import tpu as pltpu
from jax.sharding import PartitionSpec as P

AXES = ("rep", "fsdp")
SHARE = 1.33 / 8
UPPER = ((4, 7, 5, 6), (4, 5, 6, 7))
LOWER = (((0, 1, 3, 2), (3, 1, 2, 0)), ((3, 2, 1, 0), (0, 1, 2, 3)))


def spot(rep, col, core):
    return rep * 16 + col * 2 + core


def holder(block, col, core):
    side = col // 4
    rep = UPPER[side][block - 4] if block >= 4 else LOWER[side][core][block]
    return spot(rep, col, core)


LINE = [
    [holder(block, c, k) for y in range(4) for block in (4 + y, y) for k in (1, 0)] for c in range(8)
]
TO_HOLDER = [
    (spot(c, block, k), holder(block, c, k)) for block in range(8) for c in range(8) for k in range(2)
]
TO_OWNER = [(b, a) for a, b in TO_HOLDER]


def rounded(x):
    return lax.reduce_precision(x, 8, 7).astype(jnp.bfloat16)


def swap_rows(x):
    return lax.all_to_all(x, AXES, split_axis=0, concat_axis=0, tiled=True, axis_index_groups=LINE)


LISTED = [(4 * upper + y) * 2 + core for y in range(4) for upper in (1, 0) for core in (1, 0)]


PIECES = 4


def listed_kernel(rows_ref, out_ref, taken, listed, in_sems, out_sems):
    wide = rows_ref.shape[1] // PIECES
    deep = out_ref.shape[1] // PIECES
    fetches = [
        pltpu.make_async_copy(rows_ref.at[:, pl.ds(i * wide, wide)], taken.at[i], in_sems.at[i])
        for i in range(PIECES)
    ]
    stores = [
        pltpu.make_async_copy(listed.at[i], out_ref.at[:, pl.ds(i * deep, deep), :], out_sems.at[i])
        for i in range(PIECES)
    ]
    for fetch in fetches:
        fetch.start()
    for i in range(PIECES):
        fetches[i].wait()
        rows = taken[i].reshape(rows_ref.shape[0], deep, 128)
        for place, row in enumerate(LISTED):
            listed[i, place] = rows[row]
        stores[i].start()
    for store in stores:
        store.wait()


def listed_rows(rows, deep):
    anywhere = pl.BlockSpec(memory_space=pl.ANY)
    count, width = rows.shape
    return pl.pallas_call(
        listed_kernel,
        out_shape=jax.ShapeDtypeStruct((count,) + deep, rows.dtype),
        in_specs=[anywhere],
        out_specs=anywhere,
        scratch_shapes=[
            pltpu.VMEM((PIECES, count, width // PIECES), rows.dtype),
            pltpu.VMEM((PIECES, count, deep[0] // PIECES, 128), rows.dtype),
            pltpu.SemaphoreType.DMA((PIECES,)),
            pltpu.SemaphoreType.DMA((PIECES,)),
        ],
    )(rows)


def plain_kernel(listed_ref, out_ref, plain, sems):
    wide = out_ref.shape[1] // PIECES
    deep = listed_ref.shape[1] // PIECES
    stores = []
    for i in range(PIECES):
        rows = [listed_ref[LISTED.index(row), i * deep : (i + 1) * deep] for row in range(len(LISTED))]
        plain[i] = jnp.stack(rows).reshape(len(LISTED), wide)
        stores.append(
            pltpu.make_async_copy(plain.at[i], out_ref.at[:, pl.ds(i * wide, wide)], sems.at[i])
        )
        stores[-1].start()
    for store in stores:
        store.wait()


def plain_rows(listed):
    count, deep, _ = listed.shape
    listed = pltpu.with_memory_space_constraint(listed, pltpu.VMEM)
    return pl.pallas_call(
        plain_kernel,
        out_shape=jax.ShapeDtypeStruct((count, deep * 128), listed.dtype),
        in_specs=[pl.BlockSpec(memory_space=pltpu.VMEM)],
        out_specs=pl.BlockSpec(memory_space=pl.ANY),
        scratch_shapes=[
            pltpu.VMEM((PIECES, count, deep * 128 // PIECES), listed.dtype),
            pltpu.SemaphoreType.DMA((PIECES,)),
        ],
        compiler_params=pltpu.CompilerParams(vmem_limit_bytes=4 * 2**20),
    )(listed)


def fresh_kernel(got_ref, held_ref, spread_ref, sums_ref):
    f32 = jnp.float32
    for core in range(2):
        summed = got_ref[0, 1 - core].astype(f32)
        for i in range(1, 8):
            summed = summed + got_ref[i, 1 - core].astype(f32)
        sums_ref[core] = summed.astype(jnp.bfloat16)
        fresh = (held_ref[core].astype(f32) + SHARE * summed).astype(jnp.bfloat16)
        for i in range(8):
            spread_ref[i, 1 - core] = fresh


def fresh_rows(got, held):
    vmem = pl.BlockSpec(memory_space=pltpu.VMEM)
    got = pltpu.with_memory_space_constraint(got, pltpu.VMEM)
    held = pltpu.with_memory_space_constraint(held, pltpu.VMEM)
    return pl.pallas_call(
        fresh_kernel,
        out_shape=[pltpu.VMEM(got.shape, got.dtype), pltpu.VMEM(held.shape, held.dtype)],
        in_specs=[vmem] * 2,
        out_specs=[vmem] * 2,
        compiler_params=pltpu.CompilerParams(vmem_limit_bytes=4 * 2**20),
    )(got, held)


def body(local_params, global_owned, momentum):
    rows, width = local_params.shape[1:]
    deep = (width // 128, 128)
    owned = global_owned.reshape(2, *deep)
    moment = momentum.reshape(2, *deep)
    f32 = jnp.float32

    got = swap_rows(listed_rows(local_params[0], deep))
    state = rounded(-0.33 * owned - 0.567 * moment)
    held = lax.ppermute(state, AXES, TO_HOLDER)
    spread, sums = fresh_rows(got.reshape(8, 2, *deep), held)
    back = lax.ppermute(sums, AXES, TO_OWNER)
    spread = spread.reshape(rows, *deep)
    replica_params = plain_rows(swap_rows(spread))

    back, owned, moment = lax.optimization_barrier((back, owned, moment))
    pseudo = owned - back.astype(f32) / 8
    moment_new = 0.9 * moment + pseudo
    global_new = owned - 0.7 * (pseudo + 0.9 * moment_new)
    return (global_new.reshape(2, 1, width), moment_new.reshape(2, 1, width), replica_params)


def solution(mesh):
    return jax.shard_map(
        body,
        mesh=mesh,
        in_specs=(P("rep", "fsdp", "tp"), P("rep", "fsdp", "tp"), P("rep", "fsdp", "tp")),
        out_specs=(P("rep", "fsdp", "tp"), P("rep", "fsdp", "tp"), P("fsdp", "tp")),
        check_vma=False,
    )
```

```python
import jax
import jax.numpy as jnp
from jax import lax
from jax.experimental import pallas as pl
from jax.experimental.pallas import tpu as pltpu
from jax.sharding import PartitionSpec as P

AXES = ("rep", "fsdp")
SHARE = 1.33 / 8
UPPER = ((4, 7, 5, 6), (4, 5, 6, 7))
LOWER = (((0, 1, 3, 2), (3, 1, 2, 0)), ((3, 2, 1, 0), (0, 1, 2, 3)))


def spot(rep, col, core):
    return rep * 16 + col * 2 + core


def holder(block, col, core):
    side = col // 4
    rep = UPPER[side][block - 4] if block >= 4 else LOWER[side][core][block]
    return spot(rep, col, core)


LINE = [
    [holder(block, c, k) for y in range(4) for block in (4 + y, y) for k in (1, 0)] for c in range(8)
]
TO_HOLDER = [
    (spot(c, block, k), holder(block, c, k)) for block in range(8) for c in range(8) for k in range(2)
]
TO_OWNER = [(b, a) for a, b in TO_HOLDER]


def rounded(x):
    return lax.reduce_precision(x, 8, 7).astype(jnp.bfloat16)


def swap_rows(x):
    return lax.all_to_all(x, AXES, split_axis=0, concat_axis=0, tiled=True, axis_index_groups=LINE)


LISTED = [(4 * upper + y) * 2 + core for y in range(4) for upper in (1, 0) for core in (1, 0)]


PIECES = 4


def listed_kernel(rows_ref, out_ref, taken, listed, in_sems, out_sems):
    wide = rows_ref.shape[1] // PIECES
    deep = out_ref.shape[1] // PIECES
    fetches = [
        pltpu.make_async_copy(rows_ref.at[:, pl.ds(i * wide, wide)], taken.at[i], in_sems.at[i])
        for i in range(PIECES)
    ]
    stores = [
        pltpu.make_async_copy(listed.at[i], out_ref.at[:, pl.ds(i * deep, deep), :], out_sems.at[i])
        for i in range(PIECES)
    ]
    for fetch in fetches:
        fetch.start()
    for i in range(PIECES):
        fetches[i].wait()
        rows = taken[i].reshape(rows_ref.shape[0], deep, 128)
        for place, row in enumerate(LISTED):
            listed[i, place] = rows[row]
        stores[i].start()
    for store in stores:
        store.wait()


def listed_rows(rows, deep):
    anywhere = pl.BlockSpec(memory_space=pl.ANY)
    count, width = rows.shape
    return pl.pallas_call(
        listed_kernel,
        out_shape=jax.ShapeDtypeStruct((count,) + deep, rows.dtype),
        in_specs=[anywhere],
        out_specs=anywhere,
        scratch_shapes=[
            pltpu.VMEM((PIECES, count, width // PIECES), rows.dtype),
            pltpu.VMEM((PIECES, count, deep[0] // PIECES, 128), rows.dtype),
            pltpu.SemaphoreType.DMA((PIECES,)),
            pltpu.SemaphoreType.DMA((PIECES,)),
        ],
    )(rows)


def plain_kernel(listed_ref, out_ref, plain, sems):
    wide = out_ref.shape[1] // PIECES
    deep = listed_ref.shape[1] // PIECES
    stores = []
    for i in range(PIECES):
        rows = [listed_ref[LISTED.index(row), i * deep : (i + 1) * deep] for row in range(len(LISTED))]
        plain[i] = jnp.stack(rows).reshape(len(LISTED), wide)
        stores.append(
            pltpu.make_async_copy(plain.at[i], out_ref.at[:, pl.ds(i * wide, wide)], sems.at[i])
        )
        stores[-1].start()
    for store in stores:
        store.wait()


def plain_rows(listed):
    count, deep, _ = listed.shape
    listed = pltpu.with_memory_space_constraint(listed, pltpu.VMEM)
    return pl.pallas_call(
        plain_kernel,
        out_shape=jax.ShapeDtypeStruct((count, deep * 128), listed.dtype),
        in_specs=[pl.BlockSpec(memory_space=pltpu.VMEM)],
        out_specs=pl.BlockSpec(memory_space=pl.ANY),
        scratch_shapes=[
            pltpu.VMEM((PIECES, count, deep * 128 // PIECES), listed.dtype),
            pltpu.SemaphoreType.DMA((PIECES,)),
        ],
        compiler_params=pltpu.CompilerParams(vmem_limit_bytes=4 * 2**20),
    )(listed)


def fresh_kernel(got_ref, held_ref, spread_ref, sums_ref, fresh, sems):
    f32 = jnp.float32
    stores = []
    for core in range(2):
        summed = got_ref[0, 1 - core].astype(f32)
        for i in range(1, 8):
            summed = summed + got_ref[i, 1 - core].astype(f32)
        sums_ref[core] = summed.astype(jnp.bfloat16)
        fresh[core] = (held_ref[core].astype(f32) + SHARE * summed).astype(jnp.bfloat16)
        for i in range(8):
            stores.append(
                pltpu.make_async_copy(fresh.at[core], spread_ref.at[i, 1 - core], sems.at[core, i])
            )
            stores[-1].start()
    for store in stores:
        store.wait()


def fresh_rows(got, held):
    vmem = pl.BlockSpec(memory_space=pltpu.VMEM)
    got = pltpu.with_memory_space_constraint(got, pltpu.VMEM)
    held = pltpu.with_memory_space_constraint(held, pltpu.VMEM)
    return pl.pallas_call(
        fresh_kernel,
        out_shape=[jax.ShapeDtypeStruct(got.shape, got.dtype), pltpu.VMEM(held.shape, held.dtype)],
        in_specs=[vmem] * 2,
        out_specs=[pl.BlockSpec(memory_space=pl.ANY), vmem],
        scratch_shapes=[pltpu.VMEM(held.shape, held.dtype), pltpu.SemaphoreType.DMA((2, 8))],
        compiler_params=pltpu.CompilerParams(vmem_limit_bytes=4 * 2**20),
    )(got, held)


def body(local_params, global_owned, momentum):
    rows, width = local_params.shape[1:]
    deep = (width // 128, 128)
    owned = global_owned.reshape(2, *deep)
    moment = momentum.reshape(2, *deep)
    f32 = jnp.float32

    got = swap_rows(listed_rows(local_params[0], deep))
    state = rounded(-0.33 * owned - 0.567 * moment)
    held = lax.ppermute(state, AXES, TO_HOLDER)
    spread, sums = fresh_rows(got.reshape(8, 2, *deep), held)
    back = lax.ppermute(sums, AXES, TO_OWNER)
    spread = spread.reshape(rows, *deep)
    replica_params = plain_rows(swap_rows(spread))

    back, owned, moment = lax.optimization_barrier((back, owned, moment))
    pseudo = owned - back.astype(f32) / 8
    moment_new = 0.9 * moment + pseudo
    global_new = owned - 0.7 * (pseudo + 0.9 * moment_new)
    return (global_new.reshape(2, 1, width), moment_new.reshape(2, 1, width), replica_params)


def solution(mesh):
    return jax.shard_map(
        body,
        mesh=mesh,
        in_specs=(P("rep", "fsdp", "tp"), P("rep", "fsdp", "tp"), P("rep", "fsdp", "tp")),
        out_specs=(P("rep", "fsdp", "tp"), P("rep", "fsdp", "tp"), P("fsdp", "tp")),
        check_vma=False,
    )
```
